32 devices in a mesh: depth: 8 (over z, core), slab: 4 (over y, x).
Axes of the slice: x: 2, y: 2, z: 4, core: 2. Of those that a mesh axis runs over, the one named last changes fastest.
Arguments:
- state: float32 [8, 2, 2048, 2048], P('depth', None, 'slab'), may hold values from -6 to 6
- fresh: float32 [2, 2, 2048, 2048], P(None, None, 'slab'), may hold values from -6 to 6
- operators: float32 [4, 2, 2, 384, 128], replicated
- band: int32 [8], P('depth'), may hold values from 0 to 1
- freq_sched: int32 [10], replicated, may hold values from 0 to 3
Outputs:
- state_out: float32 [8, 2, 2048, 2048], P('depth', None, 'slab')
- image: float32 [8, 2048], P('depth', 'slab')
The draws below stay inside these ranges and needn't reach their ends.
All inputs are finite; a program needn't handle non-finite values.
Results may differ from the reference program's by a relative error of at most 0.00011.
Values sent between devices are 32-bit elements; how exact they have to be, the bound alone decides.
No kernel may reach another device: no remote copies, remote signals or barrier semaphores. Data moves between devices by JAX's collectives and lax.ppermute only.
A program may use at most 192 MiB of HBM per device.

```python
import math
import jax
import jax.numpy as jnp
from jax import lax

S = 2048
R = 2048
BLK = 128
NF = 4
NB = 2
TICKS = 2
NZ = 8


def covering_ids(key, length, limit):
    values = jax.random.randint(key, (length,), 0, limit)
    order = jax.random.permutation(jax.random.fold_in(key, 7), length)
    return values.at[order[:limit]].set(jnp.arange(limit, dtype=jnp.int32)).astype(jnp.int32)


def draw_band(key, part):
    return covering_ids(jax.random.fold_in(key, 11), NZ, NB)


def draw_freq_sched(key, part):
    return covering_ids(jax.random.fold_in(key, 23), TICKS + NZ, NF)


def draw_operators(key, part):
    key_noise, key_amp, key_angle = jax.random.split(jax.random.fold_in(key, 31), 3)
    spread = 0.5
    amp = jax.random.uniform(key_amp, (NF, NB, BLK), jnp.float32, 0.6, 1.0)
    noise = jax.random.normal(key_noise, (NF, NB, 2, 3 * BLK, BLK), jnp.float32) * (spread / math.sqrt(6.0 * BLK))
    angle = jax.random.uniform(key_angle, (NF, NB, BLK), jnp.float32, -math.pi, math.pi)
    parts = jnp.stack([amp * jnp.cos(angle), amp * jnp.sin(angle)], axis=2)
    middle = parts[..., None, :] * jnp.eye(BLK, dtype=jnp.float32)
    zeros = jnp.zeros((NF, NB, 2, BLK, BLK), jnp.float32)
    return noise + jnp.concatenate([zeros, middle, zeros], axis=3)


def level_of(stream_key, extent, cuts, least, top_value):
    gain, own = 1.0, jax.random.fold_in(stream_key, 6)
    for dim, shards_of in cuts:
        heights = jnp.exp(jax.random.uniform(jax.random.fold_in(own, dim), (shards_of,), jnp.float32, least / len(cuts), top_value / len(cuts)))
        gain = gain * jnp.repeat(heights, extent[dim] // shards_of).reshape([-1 if axis == dim else 1 for axis in range(len(extent))])
    return gain


def normal_values(stream_key, extent, deviation, reach, shards=(), held_as=jnp.bfloat16):
    entries = jax.random.normal(stream_key, extent, jnp.float32) * deviation
    if len(shards) > 0:
        entries = level_of(stream_key, extent, shards, -0.22, 0.18) * entries
    return jnp.clip(entries, min=-reach, max=reach).astype(held_as)


def setup_inputs(seed: int = 0) -> dict:
    keys = jax.random.split(jax.random.key(seed), 6)
    state = normal_values(keys[0], (NZ, 2, S, R), 1.0, 6.0, ((0, 8), (2, 4)), jnp.float32)
    fresh = normal_values(keys[1], (TICKS, 2, S, R), 1.0, 6.0, ((2, 4),), jnp.float32)
    operators = draw_operators(jax.random.fold_in(keys[5], 71), 0)
    band = draw_band(jax.random.fold_in(keys[5], 71), 0)
    freq_sched = draw_freq_sched(jax.random.fold_in(keys[5], 71), 0)
    return {"state": state, "fresh": fresh, "operators": operators, "band": band, "freq_sched": freq_sched}


def cmul(triple, operator, form):
    hp = lax.Precision.HIGHEST
    real_part = jnp.einsum(form, triple[0], operator[0], precision=hp) - jnp.einsum(form, triple[1], operator[1], precision=hp)
    imag_part = jnp.einsum(form, triple[0], operator[1], precision=hp) + jnp.einsum(form, triple[1], operator[0], precision=hp)
    return jnp.stack([real_part, imag_part])


def along_middle(extended, operator):
    width = operator.shape[-1]
    count = extended.shape[1] // width - 2
    blocks = extended.reshape(2, count + 2, width, extended.shape[2])
    triple = jnp.concatenate([blocks[:, :-2], blocks[:, 1:-1], blocks[:, 2:]], axis=2)
    return cmul(triple, operator, "bic,ij->bjc").reshape(2, count * width, extended.shape[2])


def along_last(field, operator):
    width = operator.shape[-1]
    count = field.shape[2] // width
    padded = jnp.pad(field, ((0, 0), (0, 0), (width, width)))
    blocks = padded.reshape(2, field.shape[1], count + 2, width)
    triple = jnp.concatenate([blocks[:, :, :-2], blocks[:, :, 1:-1], blocks[:, :, 2:]], axis=3)
    return cmul(triple, operator, "abi,ij->abj").reshape(2, field.shape[1], count * width)


def one_step(field, operator):
    width = operator.shape[-1]
    moved = along_last(field, operator)
    padded = jnp.pad(moved, ((0, 0), (width, width), (0, 0)))
    return along_middle(padded, operator)


def reference(state, fresh, operators, band, freq_sched):
    current = state
    image = jnp.zeros((NZ, S), jnp.float32)
    owners = jnp.arange(NZ, dtype=jnp.int32)
    for tick in range(TICKS):
        freq_ids = freq_sched[(TICKS - tick + owners).astype(jnp.int32)]
        chosen = operators[freq_ids, band]
        result = lax.map(lambda pair: one_step(pair[0], pair[1]), (current, chosen))
        image = image + jnp.diagonal(result[:, 0], axis1=1, axis2=2)
        current = jnp.concatenate([fresh[tick][None], result[:-1]], axis=0)
    return current, image
```

```python
import functools
import math

import jax
import jax.numpy as jnp
from jax import lax
from jax.experimental import pallas as pl
from jax.experimental.pallas import tpu as pltpu
from jax.sharding import PartitionSpec as P

BF = jnp.bfloat16
F32 = jnp.float32
VMEM = 62 << 20
AXES = ("depth", "slab")


def split(value):
    high = value.astype(BF)
    return high, (value - high.astype(F32)).astype(BF)


def params():
    return pltpu.CompilerParams(vmem_limit_bytes=VMEM)


def after(value, *others):
    return lax.optimization_barrier((value, *others))[0]


def cost():
    return pl.CostEstimate(flops=1, bytes_accessed=1, transcendentals=0)


def rows_kernel(mode, x_ref, *outs):
    @pl.when(mode[0] == 1)
    def _():
        outs[0][...] = x_ref[...]

    @pl.when(mode[0] == 2)
    def _():
        at = 0
        for ref in outs[1:]:
            ref[...] = x_ref[:, :, at : at + ref.shape[2]]
            at += ref.shape[2]


def rows_of(mode, x, blocks, width, chunks):
    cols = x.shape[-1]
    tall = width // 4
    lengths = [(1, cols)] + [(2, cols // chunks)] * chunks

    def part(wanted, length):
        return pl.BlockSpec((2, tall, length), lambda i, mode: (0, jnp.where(mode[0] == wanted, i, 0), 0))

    return pl.pallas_call(
        rows_kernel,
        grid_spec=pltpu.PrefetchScalarGridSpec(
            num_scalar_prefetch=1,
            grid=(4 * blocks,),
            in_specs=[
                pl.BlockSpec(
                    (None, 2, tall, cols),
                    lambda i, mode: (0, 0, 4 * mode[1] + jnp.where(mode[0] > 0, i, 0), 0),
                )
            ],
            out_specs=[part(*item) for item in lengths],
        ),
        out_shape=[jax.ShapeDtypeStruct((2, blocks * width, length), F32) for _, length in lengths],
        compiler_params=params(),
        cost_estimate=cost(),
    )(mode, x)


def receivers_kernel(mode, *refs, width, nb, group, sources, chunks):
    inputs, (w_ref,), outs = refs[:sources], refs[sources : sources + 1], refs[sources + 1 : sources + 1 + chunks]
    xh, xl, zh, zl = refs[sources + 1 + chunks :]
    rows = inputs[0].shape[1]
    wide = 2 * width
    m = group * rows

    def product(high, low, g, step):
        hi = [high[g * group + t : g * group + t + group].reshape(m, wide) for t in range(3)]
        lo = [low[g * group + t : g * group + t + group].reshape(m, wide) for t in range(3)]
        left = jnp.concatenate(hi + lo + hi, axis=1)
        return jnp.dot(left, w_ref[step], preferred_element_type=F32).reshape(group, rows, wide)

    @pl.when(mode[0] > 0)
    def _():
        zero = jnp.zeros((1, rows, wide), BF)
        for buffer in (xh, xl, zh, zl):
            buffer[0:1] = zero
            buffer[nb + 1 : nb + 2] = zero
        for source, ref in enumerate(inputs):

            @pl.when(mode[0] == source + 1)
            def _(ref=ref):
                for j in range(nb):
                    for p in range(2):
                        high, low = split(ref[p, :, j * width : (j + 1) * width])
                        xh[j + 1, :, p * width : (p + 1) * width] = high
                        xl[j + 1, :, p * width : (p + 1) * width] = low

        for g in range(nb // group):
            high, low = split(product(xh, xl, g, 0))
            zh[g * group + 1 : g * group + 1 + group] = high
            zl[g * group + 1 : g * group + 1 + group] = low
        per = nb // chunks
        for g in range(nb // group):
            y = product(zh, zl, g, 1)
            for j in range(group):
                block = g * group + j
                out, at = outs[block // per], (block % per) * width
                for p in range(2):
                    out[p, :, at : at + width] = y[j, :, p * width : (p + 1) * width]


def receivers(mode, sources, weights, blocks, width, chunks):
    cols = sources[0].shape[-1]
    nb = cols // width
    group = 2 if nb % 2 == 0 else 1
    per = cols // chunks
    in_specs = []
    for number, array in enumerate(sources):
        lead = (None,) * (array.ndim - 3)

        def rows_at(i, mode, number=number, lead=lead):
            first = mode[1] if lead else 0
            return (0,) * len(lead) + (0, first + jnp.where(mode[0] == number + 1, i, 0), 0)

        in_specs.append(pl.BlockSpec((*lead, 2, width, cols), rows_at))
    in_specs.append(pl.BlockSpec(weights.shape, lambda i, mode: (0, 0, 0)))
    return pl.pallas_call(
        functools.partial(receivers_kernel, width=width, nb=nb, group=group, sources=len(sources), chunks=chunks),
        grid_spec=pltpu.PrefetchScalarGridSpec(
            num_scalar_prefetch=1,
            grid=(blocks,),
            in_specs=in_specs,
            out_specs=[pl.BlockSpec((2, width, per), lambda i, mode: (0, jnp.where(mode[0] > 0, i, 0), 0))] * chunks,
            scratch_shapes=[pltpu.VMEM((nb + 2, width, 2 * width), BF)] * 4,
        ),
        out_shape=[jax.ShapeDtypeStruct((2, blocks * width, per), F32)] * chunks,
        compiler_params=params(),
        cost_estimate=cost(),
    )(mode, *sources, weights)


def shots_body(mode, groups, vh_ref, vl_ref, xh, xl, store, width, nb):
    wide = 2 * width
    for number, ref in enumerate(groups):
        for b in range(ref.shape[1] // width):
            for p in range(2):
                high, low = split(ref[p, b * width : (b + 1) * width])
                at = pl.multiple_of((mode[1 + number] + b) * wide + p * width, width)
                xh[pl.ds(at, width)] = high
                xl[pl.ds(at, width)] = low
    for b in range(nb):
        centre = 5 if b == 0 else (6 if b == nb - 1 else 2)
        order = (0, 1, centre, 3, 4)
        high = [vh_ref[k] for k in order]
        low = [vl_ref[k] for k in order]
        left = jnp.concatenate(high + high + low, axis=1)
        h = xh[b * wide : (b + 5) * wide]
        l = xl[b * wide : (b + 5) * wide]
        y = jnp.dot(left, jnp.concatenate([h, l, h], axis=0), preferred_element_type=F32)
        store(b, y)


def shots_kernel(mode, *refs, width, nb, count, fresh):
    groups, rest = refs[:count], refs[count:]
    vh_ref, vl_ref, top_ref = rest[:3]
    o_ref, xh, xl = rest[-3:]

    def store(b, y):
        y = y * top_ref[0:1, 0:1] * top_ref[1:2, 0:1]
        for p in range(2):
            o_ref[p, b * width : (b + 1) * width] = y[p * width : (p + 1) * width]

    @pl.when(mode[0] == 1)
    def _():
        shots_body(mode, groups, vh_ref, vl_ref, xh, xl, store, width, nb)

    if fresh:

        @pl.when(mode[0] == 2)
        def _():
            o_ref[...] = rest[3][...]


def shots(mode, groups, weights, width, nb, at, length, total, fresh=None, into=None):
    vh, vl, tops = weights
    rows = nb * width
    ct = min(2 * width, length)
    start = at // ct

    def columns(array):
        first = 0 if array.shape[-1] == length else start
        lead = (None,) * (array.ndim - 3)
        return pl.BlockSpec(
            (*lead, 2, array.shape[-2], ct),
            lambda i, mode: (0,) * (len(lead) + 2) + (first + jnp.where(mode[0] == 1, i, 0),),
        )

    in_specs = [columns(array) for array in groups]
    in_specs += [pl.BlockSpec(vh.shape, lambda i, mode: (0, 0, 0))] * 2
    in_specs.append(pl.BlockSpec(tops.shape, lambda i, mode: (0, 0)))
    operands = [*groups, vh, vl, tops]
    aliases = {}
    if fresh is not None:
        in_specs.append(
            pl.BlockSpec(
                (None, 2, rows, ct),
                lambda i, mode: (fresh.shape[0] - 1, 0, 0, start + jnp.where(mode[0] == 2, i, 0)),
            )
        )
        operands.append(fresh)
    if into is not None:
        in_specs.append(pl.BlockSpec(memory_space=pl.ANY))
        operands.append(into)
        aliases = {len(operands): 0}
    return pl.pallas_call(
        functools.partial(shots_kernel, width=width, nb=nb, count=len(groups), fresh=fresh is not None),
        grid_spec=pltpu.PrefetchScalarGridSpec(
            num_scalar_prefetch=1,
            grid=(length // ct,),
            in_specs=in_specs,
            out_specs=pl.BlockSpec((2, rows, ct), lambda i, mode: (0, 0, start + jnp.where(mode[0] > 0, i, 0))),
            scratch_shapes=[pltpu.VMEM(((nb + 4) * 2 * width, ct), BF)] * 2,
        ),
        out_shape=jax.ShapeDtypeStruct((2, rows, total), F32),
        input_output_aliases=aliases,
        compiler_params=params(),
        cost_estimate=cost(),
    )(mode, *operands)


def place_kernel(mode, new_ref, old_ref, o_ref):
    @pl.when(mode[0] == 1)
    def _():
        o_ref[...] = new_ref[...]

    @pl.when(mode[0] != 1)
    def _():
        o_ref[...] = old_ref[...]


def place(mode, new, into, at):
    rows, cols = new.shape[1:]
    tall = math.gcd(rows, 32)
    start = at // tall
    return pl.pallas_call(
        place_kernel,
        grid_spec=pltpu.PrefetchScalarGridSpec(
            num_scalar_prefetch=1,
            grid=(rows // tall,),
            in_specs=[
                pl.BlockSpec((2, tall, cols), lambda i, mode: (0, jnp.where(mode[0] == 1, i, 0), 0)),
                pl.BlockSpec((2, tall, cols), lambda i, mode: (0, start, 0)),
            ],
            out_specs=pl.BlockSpec((2, tall, cols), lambda i, mode: (0, start + jnp.where(mode[0] == 1, i, 0), 0)),
        ),
        out_shape=jax.ShapeDtypeStruct(into.shape, F32),
        input_output_aliases={2: 0},
        compiler_params=params(),
        cost_estimate=cost(),
    )(mode, new, into)


def diagonal_kernel(info, x_ref, w_ref, s_ref, c_ref, o_ref, xh, xl, zh, zl, *, width, total):
    r = pl.program_id(0)
    block = info[0] + r
    wide = 2 * width

    def valid(offset):
        at = block + offset
        return ((at >= 0) & (at < total)).astype(F32)

    @pl.when(r == 0)
    def _():
        o_ref[...] = jnp.zeros(o_ref.shape, F32)

    def product(high, low, count, step):
        hi = [high[t : t + count].reshape(count * width, wide) for t in range(3)]
        lo = [low[t : t + count].reshape(count * width, wide) for t in range(3)]
        left = jnp.concatenate(hi + lo + hi, axis=1)
        return jnp.dot(left, w_ref[step], preferred_element_type=F32).reshape(count, width, wide)

    def given(z, m):
        return jnp.sum(z[:, :width] * m[0] - z[:, width:] * m[1], axis=0, keepdims=True)

    @pl.when(info[1] > 0)
    def _():
        for slot in range(9):
            at = jnp.clip(block + slot - 4, 0, total - 1) * width
            for p in range(2):
                value = x_ref[p, :, pl.ds(pl.multiple_of(at, width), width)] * valid(slot - 4)
                high, low = split(value)
                xh[slot, :, p * width : (p + 1) * width] = high
                xl[slot, :, p * width : (p + 1) * width] = low
        z1 = product(xh, xl, 7, 0)
        for offset in (-1, 0, 1):
            o_ref[0, pl.ds(r + 2 + offset, 1), :] += given(z1[offset + 3], s_ref[1 - offset]) * valid(offset)
        for slot in range(7):
            high, low = split(z1[slot] * valid(slot - 3))
            zh[slot] = high
            zl[slot] = low
        z2 = product(zh, zl, 5, 1)
        for offset in (-2, -1, 0, 1, 2):
            o_ref[1, pl.ds(r + 2 + offset, 1), :] += given(z2[offset + 2], c_ref[2 - offset]) * valid(offset)
        for which, edge in ((5, block == 0), (6, block == total - 1)):
            o_ref[1, pl.ds(r + 2, 1), :] -= jnp.where(edge, given(z2[2], c_ref[which]), 0.0)


def diagonal(info, x, weights, single, double, width):
    rows, cols = x.shape[-2:]
    nb, total = rows // width, cols // width
    return pl.pallas_call(
        functools.partial(diagonal_kernel, width=width, total=total),
        grid_spec=pltpu.PrefetchScalarGridSpec(
            num_scalar_prefetch=1,
            grid=(nb,),
            in_specs=[
                pl.BlockSpec((None, 2, width, cols), lambda i, info: (0, 0, jnp.where(info[1] > 0, i, 0), 0)),
                pl.BlockSpec(weights.shape, lambda i, info: (0, 0, 0)),
                pl.BlockSpec(single.shape, lambda i, info: (0, 0, 0, 0)),
                pl.BlockSpec(double.shape, lambda i, info: (0, 0, 0, 0)),
            ],
            out_specs=pl.BlockSpec((2, nb + 4, width), lambda i, info: (0, 0, 0)),
            scratch_shapes=[pltpu.VMEM((9, width, 2 * width), BF)] * 2 + [pltpu.VMEM((7, width, 2 * width), BF)] * 2,
        ),
        out_shape=jax.ShapeDtypeStruct((2, nb + 4, width), F32),
        compiler_params=params(),
        cost_estimate=cost(),
    )(info, x, weights, single, double)


def operators_kernel(ids, freqs, own_band, chip_band, link_bands, one_ref, two_ref, w_ref, vh_ref, vl_ref, top_ref, s_ref, c_ref, *, width, nb, ending):
    wide = 2 * width
    first_slab, last_slab = ids[1] == 0, ids[1] == ids[2] - 1
    row = lax.broadcasted_iota(jnp.int32, (width, width), 0)
    col = lax.broadcasted_iota(jnp.int32, (width, width), 1)
    unit = (row == col).astype(F32)
    taps = []
    for step, ref in enumerate((one_ref, two_ref)):
        complexes = []
        for t in range(3):
            real, imag = ref[0, t * width : (t + 1) * width], ref[1, t * width : (t + 1) * width]
            if step == 0 and ending:
                real = jnp.where(ids[0] < 2, unit if t == 1 else jnp.zeros_like(unit), real)
                imag = jnp.where(ids[0] < 2, jnp.zeros_like(unit), imag)
            if step == 0:
                s_ref[t, 0] = real
                s_ref[t, 1] = imag
            complexes.append((real, imag))
        top = jnp.zeros((1, 1), F32)
        for real, imag in complexes:
            both = jnp.maximum(jnp.abs(real), jnp.abs(imag))
            top = jnp.maximum(top, jnp.max(jnp.max(both, axis=0, keepdims=True), axis=1, keepdims=True))
        top = jnp.where(top > 0, top, 1.0)
        top_ref[step : step + 1] = jnp.broadcast_to(top, (1, width))
        scaled = []
        for t, (real, imag) in enumerate(complexes):
            full = jnp.concatenate(
                [jnp.concatenate([real, imag], axis=1), jnp.concatenate([-imag, real], axis=1)], axis=0
            )
            high, low = split(full)
            for at, value in ((t, high), (3 + t, high), (6 + t, low)):
                w_ref[step, at * wide : (at + 1) * wide] = value
            scaled.append(full / top)
        taps.append(scaled)
    pairs = {
        (a, b): jnp.dot(taps[0][a], taps[1][b], precision=lax.Precision.HIGHEST, preferred_element_type=F32)
        for a in range(3)
        for b in range(3)
    }
    five = [sum(pairs[a, d - a] for a in range(3) if 0 <= d - a < 3) for d in range(5)]
    lost_first = jnp.where(first_slab, pairs[2, 0], 0.0)
    lost_last = jnp.where(last_slab, pairs[0, 2], 0.0)
    first = five[2] - lost_first
    if nb == 1:
        first = first - lost_last
    for number, value in enumerate([*five, first, five[2] - lost_last]):
        high, low = split(value.T)
        vh_ref[number] = high
        vl_ref[number] = low
    for number, value in enumerate([*five, pairs[2, 0], pairs[0, 2]]):
        c_ref[number, 0] = value[:width, :width]
        c_ref[number, 1] = value[:width, width:]


def prepared(ids, freqs, bands, operators, width, nb, ticks, ending):
    rows = operators.shape[3]
    wide = 2 * width

    def chosen(step):
        def index(i, ids, freqs, own_band, chip_band, link_bands):
            k, odd = ids[0], ids[0] % 2 == 1
            if ending:
                freq = freqs[jnp.maximum(ticks + k - 2, ticks - 1)]
                if step == 0:
                    band = link_bands[1]
                else:
                    band = jnp.where(odd, chip_band[0], jnp.where(k == 0, own_band[0], link_bands[0]))
            else:
                freq = freqs[ticks + k]
                band = own_band[0] if step == 0 else jnp.where(odd, link_bands[0], chip_band[0])
            return freq, band, 0, 0, 0

        return pl.BlockSpec((None, None, 2, rows, width), index)

    shapes = [
        ((2, 9 * wide, wide), BF),
        ((7, wide, wide), BF),
        ((7, wide, wide), BF),
        ((2, width), F32),
        ((3, 2, width, width), F32),
        ((7, 2, width, width), F32),
    ]

    def whole(shape):
        return pl.BlockSpec(shape, lambda i, *_: (0,) * len(shape))

    return pl.pallas_call(
        functools.partial(operators_kernel, width=width, nb=nb, ending=ending),
        grid_spec=pltpu.PrefetchScalarGridSpec(
            num_scalar_prefetch=5,
            grid=(1,),
            in_specs=[chosen(0), chosen(1)],
            out_specs=[whole(shape) for shape, _ in shapes],
        ),
        out_shape=[jax.ShapeDtypeStruct(shape, dtype) for shape, dtype in shapes],
        compiler_params=params(),
        cost_estimate=cost(),
    )(ids, freqs, *bands, operators, operators)


def body(state, fresh, operators, band, freq_sched):
    nz, ns = lax.axis_size("depth"), lax.axis_size("slab")
    k, s = lax.axis_index("depth"), lax.axis_index("slab")
    rows, cols = state.shape[2:]
    width = operators.shape[-1]
    ticks = fresh.shape[0]
    nb = rows // width
    paired = ns == 4 and nb == 4
    pb = 2 if paired else nb
    parts = nb // pb
    chunks = 2 if (cols // width) % 4 == 0 else 1
    per = cols // chunks
    is_first, is_last = s == 0, s == ns - 1
    faced = jnp.where(s % 2 == 0, 1, 0) if paired else 0
    firsts = [faced * pb, (1 - faced) * pb] if paired else [0]

    odd = k % 2 == 1
    sends = odd & (k < nz - 2)
    ends = (k == 1) | ((k >= 2) & ~odd)

    def numbers(*values):
        return jnp.stack([jnp.asarray(value).astype(jnp.int32) for value in values])

    end_source = jnp.where(ends, jnp.where(k == 1, 2, 1), 0)
    end_mode = jnp.where(ends, 1, jnp.where(k == 0, 2, 0))
    take_mode = numbers(odd & (k > 1))
    passes = ~odd & (k < nz - 2)

    def flat(pairs, members):
        return [(i * ns + a, i * ns + b) for i in members for a, b in pairs]

    def move(value, pairs, members):
        return lax.ppermute(value, AXES, flat(pairs, members))

    def halos(value, members):
        up_pairs = [(i, i + 1) for i in range(ns - 1)]
        down_pairs = [(i + 1, i) for i in range(ns - 1)]
        if nb == 1:
            far_up = move(value, [(i, i + 2) for i in range(ns - 2)], members)
            far_down = move(value, [(i + 2, i) for i in range(ns - 2)], members)
            near_up = move(value, up_pairs, members)
            near_down = move(value, down_pairs, members)
            return [far_up, near_up, near_down, far_down]
        bottom, top = value[:, -2 * width :], value[:, : 2 * width]
        return [move(bottom, up_pairs, members), move(top, down_pairs, members)]

    facing = [(0, 1), (1, 0), (2, 3), (3, 2)]
    across = [(1, 2), (2, 1)]
    out_way, on_way = [(1, 3), (2, 0)], [(3, 2), (0, 1)]
    if paired:
        halo_places = [6 * faced, 6 * (1 - faced)]
    elif nb == 1:
        halo_places = [0, 1, 3, 4]
    else:
        halo_places = [0, nb + 2]
    part_places = [2 + first for first in firsts]

    senders = [i for i in range(1, nz - 2, 2)]
    enders = [i for i in range(nz) if i == 1 or (i >= 2 and i % 2 == 0)]

    chip_band = lax.ppermute(band, "depth", [(i, i ^ 1) for i in range(nz)])
    links = [(i, i + 1) for i in range(1, nz - 1, 2)]
    links += [(j, i) for i, j in links]
    skip = [(i, i + 2) for i in range(0, nz - 2, 2)]
    raw, pieces = [], []
    link_bands = None
    for p in range(parts):
        mode = after(numbers(jnp.where(passes, 1, jnp.where(sends, 2, 0)), firsts[p]), link_bands if p else chip_band)
        pieces.append(rows_of(mode, state, pb, width, chunks))
        raw.append(lax.ppermute(pieces[p][0], "depth", skip))
        if p == 0:
            link_bands = lax.ppermute(jnp.concatenate([band, after(chip_band, pieces[0][0])]), "depth", links)
    bands = (band, chip_band, link_bands)
    if paired:
        sent_halos = [[move(pieces[0][1], facing, senders), move(pieces[1][1], across, senders)]]
        relayed = [move(value, out_way, senders) for value in pieces[1][2:]]
        near = pieces[0][2:]
        if near:
            near = after(near, sent_halos[0][0])
        for value, relay in zip(near, relayed):
            sent_halos.append([move(value, facing, senders), move(relay, on_way, senders)])
    else:
        sent_halos = [halos(state[0], senders)] * chunks

    ids = numbers(k, s, ns)
    own_w, *own_v, own_single, own_double = prepared(ids, freq_sched, bands, operators, width, nb, ticks, False)
    ids = after(ids, own_w)
    end_w, *end_v, end_single, end_double = prepared(ids, freq_sched, bands, operators, width, nb, ticks, True)

    ended, ended_halos = [], [[] for _ in range(chunks)]

    def end_part(p, done):
        mode = after(numbers(end_source, firsts[p]), done)
        whole = paired and p == 0
        ended.append(receivers(mode, [raw[p], fresh], end_w, pb, width, 1 if whole else chunks))
        for c in range(chunks):
            if not paired:
                ended_halos[c] += halos(ended[p][c], enders)
            elif p == 1 and c == 0:
                ended_halos[c] += [move(ended[1][c], across, enders)]
            elif p == 1:
                ended_halos[c] += [move(move(ended[1][c], out_way, enders), on_way, enders)]
        if whole:
            near_end = move(ended[0][0], facing, enders)
            for c in range(chunks):
                ended_halos[c] += [near_end]
        return ended[p][0]

    done = end_part(0, end_w)

    out = None
    for c in range(chunks):
        mode = after(numbers(sends, 2, *halo_places), done)
        out = shots(mode, [state, *sent_halos[c]], own_v, width, nb, c * per, per, cols, into=out)
        done = out

    start = s * nb
    arrived, swath = [], out[None]
    for p in range(parts):
        mode = after(numbers(sends, p * pb), done)
        done = receivers(mode, [swath], own_w, pb, width, 1)[0]
        arrived.append(lax.ppermute(done, "depth", [(i, i + 2) for i in senders]))
        if p == 0:
            mode = after(numbers(start, True), done)
            given = diagonal(mode, state, own_w, own_single, own_double, width)
            mode = after(numbers(start, k == 0), given)
            given_fresh = diagonal(mode, fresh, end_w, end_single, end_double, width)
            done = given_fresh
        if p + 1 < parts:
            done = end_part(p + 1, done)

    out = None
    last = done
    for c in range(chunks):
        groups = [part[min(c, len(part) - 1)] for part in ended] + ended_halos[c]
        mode = after(numbers(end_mode, *part_places, *halo_places), last)
        out = shots(mode, groups, end_v, width, nb, c * per, per, cols, fresh=fresh, into=out)
        last = arrived[0]
        if c == 0:
            scale = own_v[2][0, 0] * own_v[2][1, 0]
            given = jnp.stack([given[0], given[1] * scale, given_fresh[1] * end_v[2][1, 0]])
            given = after(given, out)
            sums = given[:, 2 : nb + 2]
            for shift in sorted({e // nb for e in (-2, -1, nb, nb + 1)}):
                pairs = [(i, i + shift) for i in range(ns) if 0 <= i + shift < ns]
                low, high = max(-2, shift * nb), min(nb + 2, (shift + 1) * nb)
                got = lax.ppermute(given[:, low + 2 : high + 2], "slab", pairs)
                sums = sums.at[:, low - shift * nb : high - shift * nb].add(got)
            second = lax.ppermute(sums[1], "depth", [(i, i + 1) for i in range(nz - 1)])
    for p, value in enumerate(arrived):
        out = place(take_mode, value, out, p * pb * width)
    image = sums[0] + jnp.where(k == 0, sums[2], after(second, out))
    return out[None], image.reshape(1, rows)


def solution(mesh):
    return jax.shard_map(
        body,
        mesh=mesh,
        in_specs=(
            P("depth", None, "slab", None),
            P(None, None, "slab", None),
            P(),
            P("depth"),
            P(),
        ),
        out_specs=(P("depth", None, "slab", None), P("depth", "slab")),
        check_vma=False,
    )
```

```python
import functools
import math

import jax
import jax.numpy as jnp
from jax import lax
from jax.experimental import pallas as pl
from jax.experimental.pallas import tpu as pltpu
from jax.sharding import PartitionSpec as P

BF = jnp.bfloat16
F32 = jnp.float32
VMEM = 62 << 20
AXES = ("depth", "slab")


def split(value):
    high = value.astype(BF)
    return high, (value - high.astype(F32)).astype(BF)


def params():
    return pltpu.CompilerParams(vmem_limit_bytes=VMEM)


def after(value, *others):
    return lax.optimization_barrier((value, *others))[0]


def cost():
    return pl.CostEstimate(flops=1, bytes_accessed=1, transcendentals=0)


def rows_kernel(mode, x_ref, *outs):
    @pl.when(mode[0] == 1)
    def _():
        outs[0][...] = x_ref[...]

    @pl.when(mode[0] == 2)
    def _():
        at = 0
        for ref in outs[1:]:
            ref[...] = x_ref[:, :, at : at + ref.shape[2]]
            at += ref.shape[2]


def rows_of(mode, x, blocks, width, chunks):
    cols = x.shape[-1]
    tall = width // 2
    lengths = [(1, cols)] + [(2, cols // chunks)] * chunks

    def part(wanted, length):
        return pl.BlockSpec((2, tall, length), lambda i, mode: (0, jnp.where(mode[0] == wanted, i, 0), 0))

    return pl.pallas_call(
        rows_kernel,
        grid_spec=pltpu.PrefetchScalarGridSpec(
            num_scalar_prefetch=1,
            grid=(2 * blocks,),
            in_specs=[
                pl.BlockSpec(
                    (None, 2, tall, cols),
                    lambda i, mode: (0, 0, 2 * mode[1] + jnp.where(mode[0] > 0, i, 0), 0),
                )
            ],
            out_specs=[part(*item) for item in lengths],
        ),
        out_shape=[jax.ShapeDtypeStruct((2, blocks * width, length), F32) for _, length in lengths],
        compiler_params=params(),
        cost_estimate=cost(),
    )(mode, x)


def receivers_kernel(mode, *refs, width, nb, group, sources, chunks):
    inputs, (w_ref,), outs = refs[:sources], refs[sources : sources + 1], refs[sources + 1 : sources + 1 + chunks]
    xh, xl, zh, zl = refs[sources + 1 + chunks :]
    rows = inputs[0].shape[1]
    wide = 2 * width
    m = group * rows

    def product(high, low, g, step):
        hi = [high[g * group + t : g * group + t + group].reshape(m, wide) for t in range(3)]
        lo = [low[g * group + t : g * group + t + group].reshape(m, wide) for t in range(3)]
        left = jnp.concatenate(hi + lo + hi, axis=1)
        return jnp.dot(left, w_ref[step], preferred_element_type=F32).reshape(group, rows, wide)

    @pl.when(mode[0] > 0)
    def _():
        zero = jnp.zeros((1, rows, wide), BF)
        for buffer in (xh, xl, zh, zl):
            buffer[0:1] = zero
            buffer[nb + 1 : nb + 2] = zero
        for source, ref in enumerate(inputs):

            @pl.when(mode[0] == source + 1)
            def _(ref=ref):
                for j in range(nb):
                    for p in range(2):
                        high, low = split(ref[p, :, j * width : (j + 1) * width])
                        xh[j + 1, :, p * width : (p + 1) * width] = high
                        xl[j + 1, :, p * width : (p + 1) * width] = low

        for g in range(nb // group):
            high, low = split(product(xh, xl, g, 0))
            zh[g * group + 1 : g * group + 1 + group] = high
            zl[g * group + 1 : g * group + 1 + group] = low
        per = nb // chunks
        for g in range(nb // group):
            y = product(zh, zl, g, 1)
            for j in range(group):
                block = g * group + j
                out, at = outs[block // per], (block % per) * width
                for p in range(2):
                    out[p, :, at : at + width] = y[j, :, p * width : (p + 1) * width]


def receivers(mode, sources, weights, blocks, width, chunks):
    cols = sources[0].shape[-1]
    nb = cols // width
    group = 4 if nb % 4 == 0 else 1
    tall = width // 2
    steps = blocks * (width // tall)
    per = cols // chunks
    in_specs = []
    for number, array in enumerate(sources):
        lead = (None,) * (array.ndim - 3)

        def rows_at(i, mode, number=number, lead=lead):
            first = mode[1] * (width // tall) if lead else 0
            return (0,) * len(lead) + (0, first + jnp.where(mode[0] == number + 1, i, 0), 0)

        in_specs.append(pl.BlockSpec((*lead, 2, tall, cols), rows_at))
    in_specs.append(pl.BlockSpec(weights.shape, lambda i, mode: (0, 0, 0)))
    return pl.pallas_call(
        functools.partial(receivers_kernel, width=width, nb=nb, group=group, sources=len(sources), chunks=chunks),
        grid_spec=pltpu.PrefetchScalarGridSpec(
            num_scalar_prefetch=1,
            grid=(steps,),
            in_specs=in_specs,
            out_specs=[pl.BlockSpec((2, tall, per), lambda i, mode: (0, jnp.where(mode[0] > 0, i, 0), 0))] * chunks,
            scratch_shapes=[pltpu.VMEM((nb + 2, tall, 2 * width), BF)] * 4,
        ),
        out_shape=[jax.ShapeDtypeStruct((2, blocks * width, per), F32)] * chunks,
        compiler_params=params(),
        cost_estimate=cost(),
    )(mode, *sources, weights)


def shots_body(mode, groups, vh_ref, vl_ref, xh, xl, store, width, nb):
    wide = 2 * width
    for number, ref in enumerate(groups):
        for b in range(ref.shape[1] // width):
            for p in range(2):
                high, low = split(ref[p, b * width : (b + 1) * width])
                at = pl.multiple_of((mode[1 + number] + b) * wide + p * width, width)
                xh[pl.ds(at, width)] = high
                xl[pl.ds(at, width)] = low
    for b in range(nb):
        centre = 5 if b == 0 else (6 if b == nb - 1 else 2)
        order = (0, 1, centre, 3, 4)
        high = [vh_ref[k] for k in order]
        low = [vl_ref[k] for k in order]
        left = jnp.concatenate(high + high + low, axis=1)
        h = xh[b * wide : (b + 5) * wide]
        l = xl[b * wide : (b + 5) * wide]
        y = jnp.dot(left, jnp.concatenate([h, l, h], axis=0), preferred_element_type=F32)
        store(b, y)


def shots_kernel(mode, *refs, width, nb, count, fresh):
    groups, rest = refs[:count], refs[count:]
    vh_ref, vl_ref, top_ref = rest[:3]
    xh, xl = rest[-2:]
    o_ref, q_ref = (rest[-4], rest[-3]) if fresh else (rest[-3], None)

    def run(ref):
        def store(b, y):
            y = y * top_ref[0:1, 0:1] * top_ref[1:2, 0:1]
            for p in range(2):
                ref[p, b * width : (b + 1) * width] = y[p * width : (p + 1) * width]

        shots_body(mode, groups, vh_ref, vl_ref, xh, xl, store, width, nb)

    @pl.when(mode[0] == 1)
    def _():
        run(o_ref)

    if fresh:

        @pl.when(mode[0] == 2)
        def _():
            run(q_ref)
            o_ref[...] = rest[3][...]


def shots(mode, groups, weights, width, nb, at, length, total, fresh=None, into=None):
    vh, vl, tops = weights
    rows = nb * width
    ct = min(2 * width, length)
    start = at // ct

    def columns(array):
        first = 0 if array.shape[-1] == length else start
        lead = (None,) * (array.ndim - 3)
        return pl.BlockSpec(
            (*lead, 2, array.shape[-2], ct),
            lambda i, mode: (0,) * (len(lead) + 2) + (first + jnp.where(mode[0] > 0, i, 0),),
        )

    in_specs = [columns(array) for array in groups]
    in_specs += [pl.BlockSpec(vh.shape, lambda i, mode: (0, 0, 0))] * 2
    in_specs.append(pl.BlockSpec(tops.shape, lambda i, mode: (0, 0)))
    operands = [*groups, vh, vl, tops]
    aliases = {}
    out_specs = [pl.BlockSpec((2, rows, ct), lambda i, mode: (0, 0, start + jnp.where(mode[0] > 0, i, 0)))]
    out_shape = [jax.ShapeDtypeStruct((2, rows, total), F32)]
    if fresh is not None:
        out_specs.append(pl.BlockSpec((2, rows, ct), lambda i, mode: (0, 0, jnp.where(mode[0] == 2, i, 0))))
        out_shape.append(jax.ShapeDtypeStruct((2, rows, length), F32))
        in_specs.append(
            pl.BlockSpec(
                (None, 2, rows, ct),
                lambda i, mode: (fresh.shape[0] - 1, 0, 0, start + jnp.where(mode[0] == 2, i, 0)),
            )
        )
        operands.append(fresh)
    if into is not None:
        in_specs.append(pl.BlockSpec(memory_space=pl.ANY))
        operands.append(into)
        aliases = {len(operands): 0}
    return pl.pallas_call(
        functools.partial(shots_kernel, width=width, nb=nb, count=len(groups), fresh=fresh is not None),
        grid_spec=pltpu.PrefetchScalarGridSpec(
            num_scalar_prefetch=1,
            grid=(length // ct,),
            in_specs=in_specs,
            out_specs=out_specs,
            scratch_shapes=[pltpu.VMEM(((nb + 4) * 2 * width, ct), BF)] * 2,
        ),
        out_shape=out_shape,
        input_output_aliases=aliases,
        compiler_params=params(),
        cost_estimate=cost(),
    )(mode, *operands)


def place_kernel(mode, new_ref, old_ref, o_ref):
    @pl.when(mode[0] == 1)
    def _():
        o_ref[...] = new_ref[...]

    @pl.when(mode[0] != 1)
    def _():
        o_ref[...] = old_ref[...]


def place(mode, new, into, row, col):
    rows, cols = new.shape[1:]
    tall = math.gcd(math.gcd(rows, row), max(8, (1 << 17) // cols))
    start, across = row // tall, col // cols
    return pl.pallas_call(
        place_kernel,
        grid_spec=pltpu.PrefetchScalarGridSpec(
            num_scalar_prefetch=1,
            grid=(rows // tall,),
            in_specs=[
                pl.BlockSpec((2, tall, cols), lambda i, mode: (0, jnp.where(mode[0] == 1, i, 0), 0)),
                pl.BlockSpec((2, tall, cols), lambda i, mode: (0, start, across)),
            ],
            out_specs=pl.BlockSpec(
                (2, tall, cols), lambda i, mode: (0, start + jnp.where(mode[0] == 1, i, 0), across)
            ),
        ),
        out_shape=jax.ShapeDtypeStruct(into.shape, F32),
        input_output_aliases={2: 0},
        compiler_params=params(),
        cost_estimate=cost(),
    )(mode, new, into)


def diagonal_kernel(info, x_ref, w_ref, s_ref, c_ref, o_ref, xh, xl, zh, zl, *, width, total):
    r = pl.program_id(0)
    block = info[0] + r
    wide = 2 * width

    def valid(offset):
        at = block + offset
        return ((at >= 0) & (at < total)).astype(F32)

    @pl.when(r == 0)
    def _():
        o_ref[...] = jnp.zeros(o_ref.shape, F32)

    def product(high, low, count, step):
        hi = [high[t : t + count].reshape(count * width, wide) for t in range(3)]
        lo = [low[t : t + count].reshape(count * width, wide) for t in range(3)]
        left = jnp.concatenate(hi + lo + hi, axis=1)
        return jnp.dot(left, w_ref[step], preferred_element_type=F32).reshape(count, width, wide)

    def given(z, m):
        return jnp.sum(z[:, :width] * m[0] - z[:, width:] * m[1], axis=0, keepdims=True)

    @pl.when(info[1] > 0)
    def _():
        for slot in range(9):
            at = jnp.clip(block + slot - 4, 0, total - 1) * width
            for p in range(2):
                value = x_ref[p, :, pl.ds(pl.multiple_of(at, width), width)] * valid(slot - 4)
                high, low = split(value)
                xh[slot, :, p * width : (p + 1) * width] = high
                xl[slot, :, p * width : (p + 1) * width] = low
        z1 = product(xh, xl, 7, 0)
        for offset in (-1, 0, 1):
            o_ref[0, pl.ds(r + 2 + offset, 1), :] += given(z1[offset + 3], s_ref[1 - offset]) * valid(offset)
        for slot in range(7):
            high, low = split(z1[slot] * valid(slot - 3))
            zh[slot] = high
            zl[slot] = low
        z2 = product(zh, zl, 5, 1)
        for offset in (-2, -1, 0, 1, 2):
            o_ref[1, pl.ds(r + 2 + offset, 1), :] += given(z2[offset + 2], c_ref[2 - offset]) * valid(offset)
        for which, edge in ((5, block == 0), (6, block == total - 1)):
            o_ref[1, pl.ds(r + 2, 1), :] -= jnp.where(edge, given(z2[2], c_ref[which]), 0.0)


def diagonal(info, x, weights, single, double, width):
    rows, cols = x.shape[-2:]
    nb, total = rows // width, cols // width
    return pl.pallas_call(
        functools.partial(diagonal_kernel, width=width, total=total),
        grid_spec=pltpu.PrefetchScalarGridSpec(
            num_scalar_prefetch=1,
            grid=(nb,),
            in_specs=[
                pl.BlockSpec((None, 2, width, cols), lambda i, info: (0, 0, jnp.where(info[1] > 0, i, 0), 0)),
                pl.BlockSpec(weights.shape, lambda i, info: (0, 0, 0)),
                pl.BlockSpec(single.shape, lambda i, info: (0, 0, 0, 0)),
                pl.BlockSpec(double.shape, lambda i, info: (0, 0, 0, 0)),
            ],
            out_specs=pl.BlockSpec((2, nb + 4, width), lambda i, info: (0, 0, 0)),
            scratch_shapes=[pltpu.VMEM((9, width, 2 * width), BF)] * 2 + [pltpu.VMEM((7, width, 2 * width), BF)] * 2,
        ),
        out_shape=jax.ShapeDtypeStruct((2, nb + 4, width), F32),
        compiler_params=params(),
        cost_estimate=cost(),
    )(info, x, weights, single, double)


def operators_kernel(ids, freqs, own_band, chip_band, link_bands, one_ref, two_ref, w_ref, vh_ref, vl_ref, top_ref, s_ref, c_ref, *, width, nb, ending):
    wide = 2 * width
    first_slab, last_slab = ids[1] == 0, ids[1] == ids[2] - 1
    row = lax.broadcasted_iota(jnp.int32, (width, width), 0)
    col = lax.broadcasted_iota(jnp.int32, (width, width), 1)
    unit = (row == col).astype(F32)
    taps = []
    for step, ref in enumerate((one_ref, two_ref)):
        complexes = []
        for t in range(3):
            real, imag = ref[0, t * width : (t + 1) * width], ref[1, t * width : (t + 1) * width]
            if step == 0 and ending:
                real = jnp.where(ids[0] < 2, unit if t == 1 else jnp.zeros_like(unit), real)
                imag = jnp.where(ids[0] < 2, jnp.zeros_like(unit), imag)
            if step == 0:
                s_ref[t, 0] = real
                s_ref[t, 1] = imag
            complexes.append((real, imag))
        top = jnp.zeros((1, 1), F32)
        for real, imag in complexes:
            both = jnp.maximum(jnp.abs(real), jnp.abs(imag))
            top = jnp.maximum(top, jnp.max(jnp.max(both, axis=0, keepdims=True), axis=1, keepdims=True))
        top = jnp.where(top > 0, top, 1.0)
        top_ref[step : step + 1] = jnp.broadcast_to(top, (1, width))
        scaled = []
        for t, (real, imag) in enumerate(complexes):
            full = jnp.concatenate(
                [jnp.concatenate([real, imag], axis=1), jnp.concatenate([-imag, real], axis=1)], axis=0
            )
            high, low = split(full)
            for at, value in ((t, high), (3 + t, high), (6 + t, low)):
                w_ref[step, at * wide : (at + 1) * wide] = value
            scaled.append(full / top)
        taps.append(scaled)
    pairs = {
        (a, b): jnp.dot(taps[0][a], taps[1][b], precision=lax.Precision.HIGHEST, preferred_element_type=F32)
        for a in range(3)
        for b in range(3)
    }
    five = [sum(pairs[a, d - a] for a in range(3) if 0 <= d - a < 3) for d in range(5)]
    lost_first = jnp.where(first_slab, pairs[2, 0], 0.0)
    lost_last = jnp.where(last_slab, pairs[0, 2], 0.0)
    first = five[2] - lost_first
    if nb == 1:
        first = first - lost_last
    for number, value in enumerate([*five, first, five[2] - lost_last]):
        high, low = split(value.T)
        vh_ref[number] = high
        vl_ref[number] = low
    for number, value in enumerate([*five, pairs[2, 0], pairs[0, 2]]):
        c_ref[number, 0] = value[:width, :width]
        c_ref[number, 1] = value[:width, width:]


def prepared(ids, freqs, bands, operators, width, nb, ticks, ending):
    rows = operators.shape[3]
    wide = 2 * width

    def chosen(step):
        def index(i, ids, freqs, own_band, chip_band, link_bands):
            k, odd = ids[0], ids[0] % 2 == 1
            if ending:
                freq = freqs[jnp.maximum(ticks + k - 2, ticks - 1)]
                if step == 0:
                    band = link_bands[1]
                else:
                    band = jnp.where(odd, chip_band[0], jnp.where(k == 0, own_band[0], link_bands[0]))
            else:
                freq = freqs[ticks + k]
                band = own_band[0] if step == 0 else jnp.where(odd, link_bands[0], chip_band[0])
            return freq, band, 0, 0, 0

        return pl.BlockSpec((None, None, 2, rows, width), index)

    shapes = [
        ((2, 9 * wide, wide), BF),
        ((7, wide, wide), BF),
        ((7, wide, wide), BF),
        ((2, width), F32),
        ((3, 2, width, width), F32),
        ((7, 2, width, width), F32),
    ]

    def whole(shape):
        return pl.BlockSpec(shape, lambda i, *_: (0,) * len(shape))

    return pl.pallas_call(
        functools.partial(operators_kernel, width=width, nb=nb, ending=ending),
        grid_spec=pltpu.PrefetchScalarGridSpec(
            num_scalar_prefetch=5,
            grid=(1,),
            in_specs=[chosen(0), chosen(1)],
            out_specs=[whole(shape) for shape, _ in shapes],
        ),
        out_shape=[jax.ShapeDtypeStruct(shape, dtype) for shape, dtype in shapes],
        compiler_params=params(),
        cost_estimate=cost(),
    )(ids, freqs, *bands, operators, operators)


def body(state, fresh, operators, band, freq_sched):
    nz, ns = lax.axis_size("depth"), lax.axis_size("slab")
    k, s = lax.axis_index("depth"), lax.axis_index("slab")
    rows, cols = state.shape[2:]
    width = operators.shape[-1]
    ticks = fresh.shape[0]
    nb = rows // width
    paired = ns == 4 and nb == 4
    pb = 2 if paired else nb
    parts = nb // pb
    chunks = 2 if (cols // width) % 4 == 0 else 1
    per = cols // chunks
    is_first, is_last = s == 0, s == ns - 1
    faced = jnp.where(s % 2 == 0, 1, 0) if paired else 0
    firsts = [faced * pb, (1 - faced) * pb] if paired else [0]

    odd = k % 2 == 1
    sends = odd & (k < nz - 2)
    ends = ~odd

    def numbers(*values):
        return jnp.stack([jnp.asarray(value).astype(jnp.int32) for value in values])

    end_source = jnp.where(ends, jnp.where(k == 0, 2, 1), 0)
    end_mode = jnp.where(ends, jnp.where(k == 0, 2, 1), 0)
    take_mode = numbers(odd & (k > 1))
    passes = ~odd & (k < nz - 2)

    def flat(pairs, members):
        return [(i * ns + a, i * ns + b) for i in members for a, b in pairs]

    def move(value, pairs, members):
        return lax.ppermute(value, AXES, flat(pairs, members))

    def halos(value, members):
        up_pairs = [(i, i + 1) for i in range(ns - 1)]
        down_pairs = [(i + 1, i) for i in range(ns - 1)]
        if nb == 1:
            far_up = move(value, [(i, i + 2) for i in range(ns - 2)], members)
            far_down = move(value, [(i + 2, i) for i in range(ns - 2)], members)
            near_up = move(value, up_pairs, members)
            near_down = move(value, down_pairs, members)
            return [far_up, near_up, near_down, far_down]
        bottom, top = value[:, -2 * width :], value[:, : 2 * width]
        return [move(bottom, up_pairs, members), move(top, down_pairs, members)]

    facing = [(0, 1), (1, 0), (2, 3), (3, 2)]
    across = [(1, 2), (2, 1)]
    out_way, on_way = [(1, 3), (2, 0)], [(3, 2), (0, 1)]
    if paired:
        halo_places = [6 * faced, 6 * (1 - faced)]
    elif nb == 1:
        halo_places = [0, 1, 3, 4]
    else:
        halo_places = [0, nb + 2]
    part_places = [2 + first for first in firsts]

    senders = [i for i in range(1, nz - 2, 2)]
    enders = [i for i in range(0, nz, 2)]

    chip_band = lax.ppermute(band, "depth", [(i, i ^ 1) for i in range(nz)])
    links = [(i, i + 1) for i in range(1, nz - 1, 2)]
    links += [(j, i) for i, j in links]
    skip = [(i, i + 2) for i in range(0, nz - 2, 2)]
    raw, pieces = [], []
    link_bands = None
    for p in range(parts):
        mode = after(numbers(jnp.where(passes, 1, jnp.where(sends, 2, 0)), firsts[p]), link_bands if p else chip_band)
        pieces.append(rows_of(mode, state, pb, width, chunks))
        raw.append(lax.ppermute(pieces[p][0], "depth", skip))
        if p == 0:
            link_bands = lax.ppermute(jnp.concatenate([band, after(chip_band, pieces[0][0])]), "depth", links)
    bands = (band, chip_band, link_bands)
    if paired:
        sent_halos = [[move(pieces[0][1], facing, senders), move(pieces[1][1], across, senders)]]
        relayed = [move(value, out_way, senders) for value in pieces[1][2:]]
        near = pieces[0][2:]
        if near:
            near = after(near, sent_halos[0][0])
        for value, relay in zip(near, relayed):
            sent_halos.append([move(value, facing, senders), move(relay, on_way, senders)])
    else:
        sent_halos = [halos(state[0], senders)] * chunks

    ids = numbers(k, s, ns)
    own_w, *own_v, own_single, own_double = prepared(ids, freq_sched, bands, operators, width, nb, ticks, False)
    ids = after(ids, own_w)
    end_w, *end_v, end_single, end_double = prepared(ids, freq_sched, bands, operators, width, nb, ticks, True)

    start = s * nb
    mode = after(numbers(start, k == 0), end_w)
    given_fresh = diagonal(mode, fresh, end_w, end_single, end_double, width)

    def end_part(p, *done):
        mode = after(numbers(end_source, firsts[p]), *done)
        return receivers(mode, [raw[p], fresh], end_w, pb, width, 1 if paired and p == 0 else chunks)

    ended = [end_part(0, given_fresh)]
    done = ended[0][0]

    out = None
    for c in range(chunks):
        mode = after(numbers(sends, 2, *halo_places), done)
        (out,) = shots(mode, [state, *sent_halos[c]], own_v, width, nb, c * per, per, cols, into=out)
        done = out
    arrived, at = [], 0
    for count in [1, nb - 1] if nb > 1 else [nb]:
        value = receivers(after(numbers(sends, at), done), [out[None]], own_w, count, width, 1)[0]
        arrived.append((at, lax.ppermute(value, "depth", [(i, i + 2) for i in senders])))
        done = value
        if at == 0 and paired:
            near_end = move(after(ended[0][0], done), facing, enders)
        at += count

    ended_halos = [[] for _ in range(chunks)]
    if paired:
        ended.append(end_part(1, done, arrived[0][1]))
        done = ended[1][0]
        for c in range(chunks):
            value = ended[1][c]
            crossed = move(value, across, enders) if c == 0 else move(move(value, out_way, enders), on_way, enders)
            ended_halos[c] = [near_end, crossed]
    else:
        ended_halos = [halos(value, enders) for value in ended[0]]

    given = diagonal(after(numbers(start, True), done), state, own_w, own_single, own_double, width)

    out, last, crossing = None, given, []
    for c in range(chunks):
        groups = [part[min(c, len(part) - 1)] for part in ended] + ended_halos[c]
        mode = after(numbers(end_mode, *part_places, *halo_places), last)
        out, ready = shots(mode, groups, end_v, width, nb, c * per, per, cols, fresh=fresh, into=out)
        crossing.append(lax.ppermute(ready, "depth", [(0, 1)]))
        last = arrived[0][1]

    scale = own_v[2][0, 0] * own_v[2][1, 0]
    given = jnp.stack([given[0], given[1] * scale, given_fresh[1] * end_v[2][1, 0]])
    given = after(given, out)
    sums = given[:, 2 : nb + 2]
    for shift in sorted({e // nb for e in (-2, -1, nb, nb + 1)}):
        pairs = [(i, i + shift) for i in range(ns) if 0 <= i + shift < ns]
        low, high = max(-2, shift * nb), min(nb + 2, (shift + 1) * nb)
        got = lax.ppermute(given[:, low + 2 : high + 2], "slab", pairs)
        sums = sums.at[:, low - shift * nb : high - shift * nb].add(got)
    second = lax.ppermute(sums[1], "depth", [(i, i + 1) for i in range(nz - 1)])

    for c, value in enumerate(crossing):
        out = place(numbers(k == 1), value, out, 0, c * per)
    for at, value in arrived:
        out = place(take_mode, value, out, at * width, 0)
    image = sums[0] + jnp.where(k == 0, sums[2], after(second, out))
    return out[None], image.reshape(1, rows)


def solution(mesh):
    return jax.shard_map(
        body,
        mesh=mesh,
        in_specs=(
            P("depth", None, "slab", None),
            P(None, None, "slab", None),
            P(),
            P("depth"),
            P(),
        ),
        out_specs=(P("depth", None, "slab", None), P("depth", "slab")),
        check_vma=False,
    )
```
